32 devices in a mesh: db: 16 (over z, y, x), seq: 2 (over core).
Axes of the slice: x: 2, y: 2, z: 4, core: 2. Of those that a mesh axis runs over, the one named last changes fastest.
Arguments:
- reader: bfloat16 [16, 256, 2048], P('db', 'seq'), may hold values from -6 to 6
- reader_gain: float32 [2048], replicated, may hold values from 0.1 to 1.9
- database: bfloat16 [512, 8, 896], P('db')
- encoder_gain: float32 [896], replicated, may hold values from 0.1 to 1.9
- w_expand: bfloat16 [896, 1792], P('db', 'seq'), may hold values from -0.1875 to 0.1875
- w_reduce: bfloat16 [1792, 896], P('seq', 'db'), may hold values from -0.125 to 0.125
- w_query: bfloat16 [2048, 2048], P('db', 'seq'), may hold values from -0.125 to 0.125
- w_key: bfloat16 [896, 2048], P('db', 'seq'), may hold values from -0.1875 to 0.1875
- w_value: bfloat16 [896, 2048], P('db', 'seq'), may hold values from -0.1875 to 0.1875
- w_output: bfloat16 [2048, 2048], P('db', 'seq'), may hold values from -0.125 to 0.125
- neighbour_ids: int32 [16, 2, 4], replicated, may hold values from 0 to 31
- lengths: int32 [16, 2, 4], P('db'), may hold values from 1 to 128, 320 in all within a row
- owners: int32 [16, 2, 4], P('db'), may hold values from 0 to 15
Outputs:
- updated: bfloat16 [16, 256, 2048], P('db', None, 'seq')
The draws below stay inside these ranges and needn't reach their ends.
Inputs may be any that keep to these rules, and one draw needn't show every extreme that they name: For every sequence b and every q, the lengths[b, q, :] of its 4 neighbours sum to exactly 320, and the longest of them is 128.
All inputs are finite; a program needn't handle non-finite values.
Results may differ from the reference program's by a relative error of at most 0.0065.
The reference program's roundings to bfloat16 on the way count: a program that leaves them out, or rounds other values in their place, can miss the bound.
Values may be sent and summed in bfloat16 or wider, within the bound.
A program may use at most 64 MiB of HBM per device.

```python
import math
import jax
import jax.numpy as jnp
import numpy as np
from jax import lax

D = 2048
HEADS = 16
HD = 128
HW = 2048
DE = 896
FFH = 1792
SPAN = 64
KNN = 2
RL = 128
CH_DEV = 2
NBR_DEV = 4
PACK = 320
STRIPE = 8
ENTRIES = 32
SEQ = 256
N_DB = 16
N_SEQ = 2


def draw_database(key, part):
    first, second = jax.random.split(key, 2)
    shape = (N_DB * ENTRIES, STRIPE, DE)
    base = jax.random.normal(first, shape, jnp.float32)
    spread = jnp.exp(jax.random.uniform(second, (N_DB * ENTRIES, STRIPE, 1), jnp.float32, -0.7, 0.7))
    values = base * spread
    return jnp.clip(values, -300.0, 300.0).astype(jnp.bfloat16)


def with_ends(values, key, low, top_value):
    place = [jax.random.randint(jax.random.fold_in(key, axis), (), 0, length) for axis, length in enumerate(values.shape)]
    widest = values.shape.index(max(values.shape))
    beside = place[:widest] + [(place[widest] + 1) % values.shape[widest]] + place[widest + 1:]
    return values.at[tuple(place)].set(low).at[tuple(beside)].set(top_value)


def shard_levels(rng, dims, shards, low, high):
    def one(position, parts):
        heights = jax.random.uniform(jax.random.fold_in(jax.random.fold_in(rng, 6), position), (parts,), jnp.float32, low / len(shards), high / len(shards))
        return jnp.repeat(jnp.exp(heights), dims[position] // parts).reshape((-1,) + (1,) * (len(dims) - position - 1))

    factor_of = one(*shards[0])
    for cut in shards[1:]:
        factor_of = factor_of * one(*cut)
    return factor_of


def profile(count, total, most, lean):
    weights = [(1 << 20) // math.isqrt(rank ** lean) + 1 for rank in range(2, count + 1)]
    spare, given = total - most - (count - 1), [1] * (count - 1)
    while spare > 0:
        movable = [i for i in range(count - 1) if given[i] < most]
        mass, left = sum([weights[i] for i in movable]), spare
        for i in movable:
            extra = min(most - given[i], max(1, left * weights[i] // mass), spare)
            given[i] = given[i] + extra
            spare = spare - extra
    return np.array([most] + given)


def uneven(rng, amount, total, limit, lean):
    if amount == 2:
        one = jax.random.randint(rng, (), max(1, total - limit), min(limit, total - 1) + 1)
        return jnp.stack([one, total - one])
    sizes = jnp.asarray(profile(amount, total, limit, lean), jnp.int32)
    twos = (amount - 1) // 2
    donor, taker = sizes[1:1 + 2 * twos:2], sizes[2:2 + 2 * twos:2]
    room = jnp.minimum(donor - 1, limit - taker)
    shifted = jax.random.randint(jax.random.fold_in(rng, 1), (twos,), 0, 1 << 20) % (room + 1)
    sizes = sizes.at[1:1 + 2 * twos:2].set(donor - shifted).at[2:2 + 2 * twos:2].set(taker + shifted)
    return sizes[jax.random.permutation(jax.random.fold_in(rng, 2), amount)]


def gaussian(stream_key, dims, deviation, reach, cuts=(), kind=jnp.bfloat16):
    drawn = deviation * jax.random.normal(stream_key, dims, jnp.float32)
    if cuts:
        drawn = drawn * shard_levels(stream_key, dims, cuts, -0.22, 0.18)
    return jnp.clip(drawn, -reach, reach).astype(kind)


def setup_inputs(seed: int = 0) -> dict:
    keys = jax.random.split(jax.random.key(seed), 14)
    reader = gaussian(keys[0], (N_DB, SEQ, D), 1.0, 6.0, ((0, 16), (1, 2)))
    reader_gain = jnp.clip(1.0 + 0.18 * jax.random.normal(keys[1], (D,), jnp.float32), 0.1, 1.9)
    database = draw_database(jax.random.fold_in(keys[13], 71), 0)
    encoder_gain = jnp.clip(1.0 + 0.18 * jax.random.normal(keys[3], (DE,), jnp.float32), 0.1, 1.9)
    w_expand = gaussian(keys[4], (DE, FFH), DE ** -0.5, 0.1875, ((0, 16), (1, 2)))
    w_reduce = gaussian(keys[5], (FFH, DE), FFH ** -0.5, 0.125, ((0, 2), (1, 16)))
    w_query = gaussian(keys[6], (D, HW), D ** -0.5, 0.125, ((0, 16), (1, 2)))
    w_key = gaussian(keys[7], (DE, HW), DE ** -0.5, 0.1875, ((0, 16), (1, 2)))
    w_value = gaussian(keys[8], (DE, HW), DE ** -0.5, 0.1875, ((0, 16), (1, 2)))
    w_output = gaussian(keys[9], (HW, D), HW ** -0.5, 0.125, ((0, 16), (1, 2)))
    neighbour_ids = with_ends(jax.random.randint(keys[10], (N_DB, N_SEQ, NBR_DEV), 0, ENTRIES), jax.random.fold_in(keys[10], 1), 0, ENTRIES - 1).astype(jnp.int32)
    lengths = jax.vmap(lambda own: uneven(own, NBR_DEV, PACK, RL, 2))(jax.random.split(keys[11], N_DB * N_SEQ)).reshape((N_DB, N_SEQ, NBR_DEV)).astype(jnp.int32)
    owners = with_ends(jax.random.randint(keys[12], (N_DB, N_SEQ, NBR_DEV), 0, N_DB), jax.random.fold_in(keys[12], 1), 0, N_DB - 1).astype(jnp.int32)
    return dict(reader=reader, reader_gain=reader_gain, database=database, encoder_gain=encoder_gain, w_expand=w_expand, w_reduce=w_reduce, w_query=w_query, w_key=w_key, w_value=w_value, w_output=w_output, neighbour_ids=neighbour_ids, lengths=lengths, owners=owners)


epsilon = 1e-06

def rms_scale(values, scales):
    widened = values.astype(jnp.float32)
    mean_square = lax.optimization_barrier(jnp.mean(widened * widened, axis=-1, keepdims=True))
    return widened * lax.rsqrt(mean_square + epsilon) * scales

def encode_rows(stored, encoder_gain, w_expand, w_reduce, w_pairs):
    normed = rms_scale(stored, encoder_gain).astype(jnp.bfloat16)
    hidden = jax.nn.gelu(jnp.dot(normed, w_expand, preferred_element_type=jnp.float32), approximate=False).astype(jnp.bfloat16)
    encoded = (stored.astype(jnp.float32) + jnp.dot(hidden, w_reduce, preferred_element_type=jnp.float32)).astype(jnp.bfloat16)
    return jnp.dot(encoded, w_pairs, preferred_element_type=jnp.float32).astype(jnp.bfloat16)

def attend(queries, key_value, allowed):
    count = queries.shape[0]
    keys_total = key_value.shape[0]
    query_heads = queries.reshape(count, HEADS, HD).astype(jnp.float32)
    key_heads = key_value[:, :HW].reshape(keys_total, HEADS, HD).astype(jnp.float32)
    value_heads = key_value[:, HW:].reshape(keys_total, HEADS, HD).astype(jnp.float32)
    scores = jnp.einsum('qhd,khd->hqk', query_heads, key_heads) * HD ** (-0.5)
    masked = jnp.where(allowed[None], scores, -jnp.inf)
    largest = lax.optimization_barrier(jnp.max(masked, axis=-1, keepdims=True))
    largest = jnp.where(jnp.isfinite(largest), largest, 0.0)
    powers = jnp.exp(masked - largest)
    totals = lax.optimization_barrier(jnp.sum(powers, axis=-1, keepdims=True))
    weights = (powers / jnp.where(totals > 0, totals, 1.0)).astype(jnp.bfloat16)
    attended = jnp.einsum('hqk,khd->qhd', weights.astype(jnp.float32), value_heads)
    return attended.reshape(count, HW).astype(jnp.bfloat16)

def reference(reader, reader_gain, database, encoder_gain, w_expand, w_reduce, w_query, w_key, w_value, w_output, neighbour_ids, lengths, owners):
    w_pairs = jnp.concatenate([w_key, w_value], axis=1)
    stored = database.reshape(N_DB, ENTRIES * STRIPE, DE)

    def encode_block(block):
        return encode_rows(block, encoder_gain, w_expand, w_reduce, w_pairs)
    table_pairs = lax.map(encode_block, stored).reshape(N_DB * ENTRIES, STRIPE, 2 * HW)
    positions = jnp.arange(RL, dtype=jnp.int32)
    window = KNN * RL
    spans_total = N_SEQ * CH_DEV

    def one_sequence(item):
        tokens, ids_rows, length_rows, owner_rows = item
        ids_flat = ids_rows.reshape(-1).astype(jnp.int32)
        length_flat = length_rows.reshape(-1).astype(jnp.int32)
        owner_flat = owner_rows.reshape(-1).astype(jnp.int32)
        shard = (owner_flat[:, None] + positions[None, :] // STRIPE) % N_DB
        row_select = shard * ENTRIES + ids_flat[:, None]
        gathered = table_pairs[row_select, (positions % STRIPE)[None, :]]
        live = positions[None, :] < length_flat[:, None]
        span_pairs = gathered.reshape(spans_total, window, 2 * HW)
        span_live = live.reshape(spans_total, window)
        prior_pairs = jnp.concatenate([jnp.zeros((1, window, 2 * HW), jnp.bfloat16), span_pairs[:-1]], axis=0)
        prior_live = jnp.concatenate([jnp.zeros((1, window), bool), span_live[:-1]], axis=0)
        normed = rms_scale(tokens, reader_gain).astype(jnp.bfloat16)
        queries = jnp.dot(normed, w_query, preferred_element_type=jnp.float32).astype(jnp.bfloat16)
        query_spans = queries.reshape(spans_total, SPAN, HW)
        allowed = jnp.broadcast_to(prior_live[:, None, :], (spans_total, SPAN, window))
        attended = jax.vmap(attend)(query_spans, prior_pairs, allowed).reshape(SEQ, HW)
        update = jnp.dot(attended, w_output, preferred_element_type=jnp.float32)
        return (tokens.astype(jnp.float32) + update).astype(jnp.bfloat16)
    return lax.map(one_sequence, (reader, neighbour_ids, lengths, owners))
```

```python
import functools
import math

import jax
import jax.numpy as jnp
from jax import lax
from jax.experimental import pallas as pl
from jax.experimental.pallas import tpu as pltpu
from jax.sharding import PartitionSpec as P

HD = 128
SPAN = 64
KNN = 2


epsilon = 1e-06


def rms_scale(values, scales):
    widened = values.astype(jnp.float32)
    mean_square = jnp.mean(widened * widened, axis=-1, keepdims=True)
    return widened * lax.rsqrt(mean_square + epsilon) * scales


def general_body(
    reader,
    reader_gain,
    database,
    encoder_gain,
    w_expand,
    w_reduce,
    w_query,
    w_key,
    w_value,
    w_output,
    neighbour_ids,
    lengths,
    owners,
):
    shards = lax.axis_size("db")
    seq_index = lax.axis_index("seq")
    entries, stripe, features = database.shape
    query_part = lax.all_gather(w_query, "db", axis=0, tiled=True)
    reader_output_part = lax.all_gather(w_output, "db", axis=0, tiled=True)
    rows = lax.all_gather(reader[0], "seq", axis=0, tiled=True)
    normed_tokens = rms_scale(rows, reader_gain).astype(jnp.bfloat16)
    queries = jnp.dot(normed_tokens, query_part, preferred_element_type=jnp.float32).astype(
        jnp.bfloat16
    )
    rows, queries, output_part = (rows, queries, reader_output_part)
    expand_part = lax.all_gather(w_expand, "db", axis=0, tiled=True)
    reduce_part = lax.all_gather(w_reduce, "db", axis=1, tiled=True)
    key_part = lax.all_gather(w_key, "db", axis=0, tiled=True)
    value_part = lax.all_gather(w_value, "db", axis=0, tiled=True)
    stored = database.reshape(entries * stripe, features)
    normed_rows = rms_scale(stored, encoder_gain).astype(jnp.bfloat16)
    hidden = jax.nn.gelu(
        jnp.dot(normed_rows, expand_part, preferred_element_type=jnp.float32), approximate=False
    ).astype(jnp.bfloat16)
    partial_sum = jnp.dot(hidden, reduce_part, preferred_element_type=jnp.float32)
    total = lax.psum(partial_sum, "seq")
    encoded = (stored.astype(jnp.float32) + total).astype(jnp.bfloat16)
    w_pairs = jnp.concatenate([key_part, value_part], axis=1)
    table = jnp.dot(encoded, w_pairs, preferred_element_type=jnp.float32).astype(jnp.bfloat16)
    table = table.reshape(entries, stripe, w_pairs.shape[1])
    requests = neighbour_ids.reshape(shards, -1)
    chosen = jax.nn.one_hot(requests, entries, dtype=jnp.bfloat16)
    outgoing = jnp.einsum(
        "brn,nsw->brsw", chosen, table, preferred_element_type=jnp.float32
    ).astype(jnp.bfloat16)
    outgoing = outgoing.reshape(-1, stripe, w_pairs.shape[1])
    arrived = lax.all_to_all(outgoing.reshape(shards, -1, stripe, w_pairs.shape[1]), "db", split_axis=0, concat_axis=0, tiled=True)
    seq_len = rows.shape[0]
    per_seq = neighbour_ids.shape[1] * neighbour_ids.shape[2]
    width = arrived.shape[-1]
    local_heads = width // (2 * HD)
    positions = jnp.arange(stripe * shards, dtype=jnp.int32)
    owner_flat = owners[0].reshape(-1)
    length_flat = lengths[0].reshape(-1)
    source = (owner_flat[:, None] + positions[None, :] // stripe) % shards
    neighbour_index = jnp.arange(per_seq, dtype=jnp.int32)[:, None]
    flat_index = (source * per_seq + neighbour_index) * stripe + (positions % stripe)[None, :]
    key_value = arrived.reshape(-1, width)[flat_index]
    live = positions[None, :] < length_flat[:, None]
    spans = per_seq // KNN
    window = KNN * positions.shape[0]
    span_pairs = key_value.reshape(spans, window, width)
    span_live = live.reshape(spans, window)
    prior_pairs = jnp.concatenate(
        [jnp.zeros((1, window, width), jnp.bfloat16), span_pairs[:-1]], axis=0
    )
    prior_live = jnp.concatenate([jnp.zeros((1, window), bool), span_live[:-1]], axis=0)
    query_spans = queries.reshape(spans, SPAN, local_heads, HD)
    key_heads = prior_pairs[:, :, : local_heads * HD].reshape(spans, window, local_heads, HD)
    value_heads = prior_pairs[:, :, local_heads * HD :].reshape(spans, window, local_heads, HD)
    scores = jnp.einsum(
        "cqhd,ckhd->chqk", query_spans, key_heads, preferred_element_type=jnp.float32
    ) * HD ** (-0.5)
    masked = jnp.where(prior_live[:, None, None, :], scores, -jnp.inf)
    largest = jnp.max(masked, axis=-1, keepdims=True)
    largest = jnp.where(jnp.isfinite(largest), largest, 0.0)
    powers = jnp.exp(masked - largest)
    totals = jnp.sum(powers, axis=-1, keepdims=True)
    weights = (powers / jnp.where(totals > 0, totals, 1.0)).astype(jnp.bfloat16)
    attended = jnp.einsum(
        "chqk,ckhd->cqhd", weights, value_heads, preferred_element_type=jnp.float32
    )
    attended = attended.reshape(seq_len, local_heads * HD).astype(jnp.bfloat16)
    model_cols = output_part.shape[1]
    update = jnp.dot(
        lax.all_gather(attended, "seq", axis=1, tiled=True),
        output_part,
        preferred_element_type=jnp.float32,
    )
    residual = lax.dynamic_slice_in_dim(rows, seq_index * model_cols, model_cols, 1)
    result = (residual.astype(jnp.float32) + update).astype(jnp.bfloat16)
    return result[None]


MESH = pl.DeviceIdType.MESH
ZS, YS, XS = 4, 2, 2
PLANE = YS * XS
LIMIT = 56 * 1024 * 1024


def remote(src, dst, send_sem, recv_sem, chip, core):
    return pltpu.make_async_remote_copy(
        src_ref=src,
        dst_ref=dst,
        send_sem=send_sem,
        recv_sem=recv_sem,
        device_id=(chip, core),
        device_id_type=MESH,
    )


def enter(chip, core, shards):
    barrier = pltpu.get_barrier_semaphore()
    for step in range(1, shards):
        pl.semaphore_signal(
            barrier, inc=1, device_id=(lax.rem(chip + step, shards), core), device_id_type=MESH
        )
    pl.semaphore_signal(barrier, inc=1, device_id=(chip, 1 - core), device_id_type=MESH)
    pl.semaphore_wait(barrier, shards)


def gather_kernel(
    ids, reader, database, encoder_w, pair_w, query_w, output_w,
    rows_out, arrived, encoder_all, pair_all, query_all, output_all,
    outgoing, z_send, z_recv, f_send, f_recv, s_send, s_recv,
    row_send, row_recv, pass_send, pass_recv, local_sem,
):
    shards = ZS * PLANE
    chip = lax.axis_index("db")
    core = lax.axis_index("seq")
    z, y, x = chip // PLANE, lax.rem(chip // XS, YS), lax.rem(chip, XS)

    def at(zz, yy, xx):
        return zz * PLANE + yy * XS + xx

    enter(chip, core, shards)

    shares = (encoder_w, pair_w, query_w, output_w)
    wholes = (encoder_all.at[core], pair_all, query_all, output_all)
    pieces = []
    for number, share in enumerate(shares):
        cut = share.shape[0] // 32 * 16
        pieces.append((number, 0, cut, True))
        pieces.append((number, cut, share.shape[0] - cut, False))

    def place(p, zz, yy, xx):
        number, low, count, _ = pieces[p]
        return wholes[number].at[zz, yy, xx, pl.ds(low, count)]

    def source(p):
        number, low, count, _ = pieces[p]
        return shares[number].at[pl.ds(low, count)]

    def line(p, yy, xx):
        number, low, count, _ = pieces[p]
        return wholes[number].at[:, yy, xx, pl.ds(low, count)]

    def peers(p):
        if pieces[p][3]:
            return (1 - y, x), (y, 1 - x)
        return (y, 1 - x), (1 - y, x)

    def along_z(p, step):
        return remote(
            source(p), place(p, z, y, x), z_send.at[p, step - 1], z_recv.at[p, step - 1],
            at(lax.rem(z + step, ZS), y, x), core,
        )

    def from_z(p, step):
        slot = place(p, lax.rem(z + ZS - step, ZS), y, x)
        return remote(slot, slot, z_send.at[p, step - 1], z_recv.at[p, step - 1], chip, 1 - core)

    def first(p, mine):
        here = (y, x) if mine else peers(p)[0]
        slots = line(p, *here)
        return remote(slots, slots, f_send.at[p], f_recv.at[p], at(z, *peers(p)[0]), core)

    def second(p, which, mine):
        toward = peers(p)[1]
        here = [(y, x), peers(p)[0]][which] if mine else [toward, (1 - y, 1 - x)][which]
        slots = line(p, *here)
        return remote(slots, slots, s_send.at[p, which], s_recv.at[p, which], at(z, *toward), core)

    own = []
    for number, share in enumerate(shares):
        copy = pltpu.make_async_copy(share, wholes[number].at[z, y, x], local_sem.at[number])
        copy.start()
        own.append(copy)
    kept = pltpu.make_async_copy(reader, rows_out.at[core], local_sem.at[4])
    kept.start()
    passed = remote(reader, rows_out.at[core], pass_send.at[0], pass_recv.at[0], chip, 1 - core)
    passed.start()

    for p in range(len(pieces)):
        for step in range(1, ZS):
            along_z(p, step).start()
        if p == 0:
            per_row = ids.shape[0] // (2 * shards)
            for b in range(shards):
                base = (b * 2 + core) * per_row
                for m in range(per_row // KNN):
                    both = [database[ids[base + m * KNN + j]] for j in range(KNN)]
                    outgoing[b, m] = jnp.concatenate(both, axis=0)
            for step in range(1, shards):
                to = lax.rem(chip + step, shards)
                remote(
                    outgoing.at[to], arrived.at[:, chip], row_send.at[step - 1],
                    row_recv.at[step - 1], to, core,
                ).start()
            mine = pltpu.make_async_copy(outgoing.at[chip], arrived.at[:, chip], local_sem.at[5])
            mine.start()

    for copy in own:
        copy.wait()
    for p in range(len(pieces) + 1):
        if p < len(pieces):
            for step in range(1, ZS):
                from_z(p, step).wait_recv()
            first(p, True).start()
            second(p, 0, True).start()
        if p > 0:
            first(p - 1, False).wait_recv()
            second(p - 1, 1, True).start()
    whole = encoder_all.at[core]
    for p in range(len(pieces)):
        for which in range(2):
            second(p, which, False).wait_recv()
        if p == 1:
            remote(whole, whole, pass_send.at[1], pass_recv.at[1], chip, 1 - core).start()

    for p in range(len(pieces)):
        for step in range(1, ZS):
            along_z(p, step).wait_send()
        first(p, True).wait_send()
        for which in range(2):
            second(p, which, True).wait_send()
    for step in range(1, shards):
        sender = lax.rem(chip + shards - step, shards)
        landed = remote(
            outgoing.at[sender], arrived.at[:, sender], row_send.at[step - 1],
            row_recv.at[step - 1], sender, core,
        )
        landed.wait_send()
        landed.wait_recv()
    mine.wait()
    kept.wait()
    other = rows_out.at[1 - core]
    taken = remote(other, other, pass_send.at[0], pass_recv.at[0], chip, 1 - core)
    taken.wait_send()
    taken.wait_recv()
    other = encoder_all.at[1 - core]
    taken = remote(other, other, pass_send.at[1], pass_recv.at[1], chip, 1 - core)
    taken.wait_send()
    taken.wait_recv()


def gather_all(ids, reader, database, encoder_w, pair_w, query_w, output_w):
    shards = ZS * PLANE
    bf16 = jnp.bfloat16
    features = database.shape[-1]
    per_row = ids.shape[0] // (2 * shards)
    spans = per_row // KNN
    stripes = KNN * database.shape[1]

    def whole(share):
        return jax.ShapeDtypeStruct((ZS, YS, XS) + share.shape, bf16)

    vmem, smem = pl.BlockSpec(memory_space=pltpu.VMEM), pl.BlockSpec(memory_space=pltpu.SMEM)
    hbm = pl.BlockSpec(memory_space=pl.ANY)
    dma = pltpu.SemaphoreType.DMA
    return pl.pallas_call(
        gather_kernel,
        out_shape=(
            jax.ShapeDtypeStruct((2,) + reader.shape, bf16),
            jax.ShapeDtypeStruct((spans, shards, stripes, features), bf16),
            jax.ShapeDtypeStruct((2, ZS, YS, XS) + encoder_w.shape, bf16),
            whole(pair_w),
            whole(query_w),
            whole(output_w),
        ),
        in_specs=[smem, hbm, vmem, hbm, hbm, hbm, hbm],
        out_specs=(hbm,) * 6,
        scratch_shapes=[
            pltpu.VMEM((shards, spans, stripes, features), bf16),
            dma((8, 3)), dma((8, 3)), dma((8,)), dma((8,)), dma((8, 2)), dma((8, 2)),
            dma((shards - 1,)), dma((shards - 1,)), dma((2,)), dma((2,)), dma((6,)),
        ],
        compiler_params=pltpu.CompilerParams(
            collective_id=0, has_side_effects=True, vmem_limit_bytes=LIMIT // 4
        ),
    )(ids, reader, database, encoder_w, pair_w, query_w, output_w)


def swap_kernel(mine, both, send_sem, recv_sem, local_sem):
    chip = lax.axis_index("db")
    core = lax.axis_index("seq")
    barrier = pltpu.get_barrier_semaphore()
    pl.semaphore_signal(barrier, inc=1, device_id=(chip, 1 - core), device_id_type=MESH)
    pl.semaphore_wait(barrier, 1)
    kept = pltpu.make_async_copy(mine, both.at[core], local_sem)
    kept.start()
    copy = remote(mine, both.at[core], send_sem, recv_sem, chip, 1 - core)
    copy.start()
    kept.wait()
    copy.wait()


def swap(mine, number):
    vmem = pl.BlockSpec(memory_space=pltpu.VMEM)
    return pl.pallas_call(
        swap_kernel,
        out_shape=jax.ShapeDtypeStruct((2,) + mine.shape, mine.dtype),
        in_specs=[vmem],
        out_specs=vmem,
        scratch_shapes=[pltpu.SemaphoreType.DMA] * 3,
        compiler_params=pltpu.CompilerParams(
            collective_id=number, has_side_effects=True, vmem_limit_bytes=LIMIT // 4
        ),
    )(mine)


def banded_body(
    reader,
    reader_gain,
    database,
    encoder_gain,
    w_expand,
    w_reduce,
    w_query,
    w_key,
    w_value,
    w_output,
    neighbour_ids,
    lengths,
    owners,
):
    f32, bf16 = jnp.float32, jnp.bfloat16
    shards = ZS * PLANE
    core = lax.axis_index("seq")
    stripe, features = database.shape[1:]
    head_cols, model_cols = w_query.shape[1], w_output.shape[1]
    band = w_expand.shape[0]
    encoder_w = jnp.concatenate([w_expand, w_reduce.T], axis=0)
    pair_w = jnp.concatenate([w_key, w_value], axis=0)
    rows, arrived, encoder_all, pair_all, query_all, output_all = gather_all(
        neighbour_ids.reshape(-1), reader[0], database, encoder_w, pair_w, w_query, w_output
    )
    rows = rows.reshape(-1, rows.shape[-1])
    encoder_all = encoder_all.reshape(2, shards, 2 * band, -1)
    stored = arrived.reshape(-1, features)
    normed_rows = rms_scale(stored, encoder_gain).astype(bf16)
    total = 0.0
    for part in range(2):
        expand = encoder_all[part, :, :band].reshape(shards * band, -1)
        reduce_t = encoder_all[part, :, band:].reshape(shards * band, -1)
        hidden = jax.nn.gelu(
            jnp.dot(normed_rows, expand, preferred_element_type=f32), approximate=False
        ).astype(bf16)
        total = total + lax.dot_general(
            hidden, reduce_t, (((1,), (1,)), ((), ())), preferred_element_type=f32
        )
    encoded = (stored.astype(f32) + total).astype(bf16)
    encoded = swap(encoded, 1).reshape(-1, features)

    spans = neighbour_ids.shape[1] * neighbour_ids.shape[2] // KNN
    window = encoded.shape[0] // spans
    encoded = encoded[: (spans - 1) * window]
    pair_all = pair_all.reshape(shards, 2 * band, -1)
    key_w = pair_all[:, :band].reshape(shards * band, -1)
    value_w = pair_all[:, band:].reshape(shards * band, -1)
    heads = head_cols // HD
    keys = jnp.dot(encoded, key_w, preferred_element_type=f32).astype(bf16)
    values = jnp.dot(encoded, value_w, preferred_element_type=f32).astype(bf16)
    normed_tokens = rms_scale(rows[SPAN:], reader_gain).astype(bf16)
    queries = jnp.dot(
        normed_tokens, query_all.reshape(-1, head_cols), preferred_element_type=f32
    ).astype(bf16)

    owner = owners[0].reshape(spans, 1, KNN, 1)
    length = lengths[0].reshape(spans, 1, KNN, 1)
    origin = jnp.arange(shards, dtype=jnp.int32)[None, :, None, None]
    offset = jnp.arange(stripe, dtype=jnp.int32)[None, None, None, :]
    position = lax.rem(origin - owner + shards, shards) * stripe + offset
    live = (position < length).reshape(spans, window)[: spans - 1]

    query_spans = queries.reshape(spans - 1, SPAN, heads, HD)
    key_heads = keys.reshape(spans - 1, window, heads, HD)
    value_heads = values.reshape(spans - 1, window, heads, HD)
    scores = jnp.einsum(
        "cqhd,ckhd->chqk", query_spans, key_heads, preferred_element_type=f32
    ) * HD ** (-0.5)
    masked = jnp.where(live[:, None, None, :], scores, -jnp.inf)
    largest = jnp.max(masked, axis=-1, keepdims=True)
    powers = jnp.exp(masked - largest)
    totals = jnp.sum(powers, axis=-1, keepdims=True)
    weights = (powers / totals).astype(bf16)
    attended = jnp.einsum("chqk,ckhd->cqhd", weights, value_heads, preferred_element_type=f32)
    attended = attended.reshape(-1, head_cols).astype(bf16)
    attended = swap(attended, 2)
    output_part = output_all.reshape(2, head_cols, model_cols)
    update = jnp.dot(attended[0], output_part[0], preferred_element_type=f32)
    update = update + jnp.dot(attended[1], output_part[1], preferred_element_type=f32)
    update = jnp.concatenate([jnp.zeros((SPAN, model_cols), f32), update], axis=0)
    residual = lax.dynamic_slice_in_dim(rows, core * model_cols, model_cols, 1)
    return (residual.astype(f32) + update).astype(bf16)[None]


def solution(mesh):
    in_specs = (
        P("db", "seq", None),
        P(),
        P("db", None, None),
        P(),
        P("db", "seq"),
        P("seq", "db"),
        P("db", "seq"),
        P("db", "seq"),
        P("db", "seq"),
        P("db", "seq"),
        P(),
        P("db", None, None),
        P("db", None, None),
    )
    out_specs = P("db", None, "seq")
    grid = (mesh.shape["db"], mesh.shape["seq"])
    body = banded_body if grid == (ZS * YS * XS, 2) else general_body
    return jax.shard_map(body, mesh=mesh, in_specs=in_specs, out_specs=out_specs, check_vma=False)
```

```python
import functools
import math

import jax
import jax.numpy as jnp
from jax import lax
from jax.experimental import pallas as pl
from jax.experimental.pallas import tpu as pltpu
from jax.sharding import PartitionSpec as P

HD = 128
SPAN = 64
KNN = 2


epsilon = 1e-06


def rms_scale(values, scales):
    widened = values.astype(jnp.float32)
    mean_square = jnp.mean(widened * widened, axis=-1, keepdims=True)
    return widened * lax.rsqrt(mean_square + epsilon) * scales


def general_body(
    reader,
    reader_gain,
    database,
    encoder_gain,
    w_expand,
    w_reduce,
    w_query,
    w_key,
    w_value,
    w_output,
    neighbour_ids,
    lengths,
    owners,
):
    shards = lax.axis_size("db")
    seq_index = lax.axis_index("seq")
    entries, stripe, features = database.shape
    query_part = lax.all_gather(w_query, "db", axis=0, tiled=True)
    reader_output_part = lax.all_gather(w_output, "db", axis=0, tiled=True)
    rows = lax.all_gather(reader[0], "seq", axis=0, tiled=True)
    normed_tokens = rms_scale(rows, reader_gain).astype(jnp.bfloat16)
    queries = jnp.dot(normed_tokens, query_part, preferred_element_type=jnp.float32).astype(
        jnp.bfloat16
    )
    rows, queries, output_part = (rows, queries, reader_output_part)
    expand_part = lax.all_gather(w_expand, "db", axis=0, tiled=True)
    reduce_part = lax.all_gather(w_reduce, "db", axis=1, tiled=True)
    key_part = lax.all_gather(w_key, "db", axis=0, tiled=True)
    value_part = lax.all_gather(w_value, "db", axis=0, tiled=True)
    stored = database.reshape(entries * stripe, features)
    normed_rows = rms_scale(stored, encoder_gain).astype(jnp.bfloat16)
    hidden = jax.nn.gelu(
        jnp.dot(normed_rows, expand_part, preferred_element_type=jnp.float32), approximate=False
    ).astype(jnp.bfloat16)
    partial_sum = jnp.dot(hidden, reduce_part, preferred_element_type=jnp.float32)
    total = lax.psum(partial_sum, "seq")
    encoded = (stored.astype(jnp.float32) + total).astype(jnp.bfloat16)
    w_pairs = jnp.concatenate([key_part, value_part], axis=1)
    table = jnp.dot(encoded, w_pairs, preferred_element_type=jnp.float32).astype(jnp.bfloat16)
    table = table.reshape(entries, stripe, w_pairs.shape[1])
    requests = neighbour_ids.reshape(shards, -1)
    chosen = jax.nn.one_hot(requests, entries, dtype=jnp.bfloat16)
    outgoing = jnp.einsum(
        "brn,nsw->brsw", chosen, table, preferred_element_type=jnp.float32
    ).astype(jnp.bfloat16)
    outgoing = outgoing.reshape(-1, stripe, w_pairs.shape[1])
    arrived = lax.all_to_all(outgoing.reshape(shards, -1, stripe, w_pairs.shape[1]), "db", split_axis=0, concat_axis=0, tiled=True)
    seq_len = rows.shape[0]
    per_seq = neighbour_ids.shape[1] * neighbour_ids.shape[2]
    width = arrived.shape[-1]
    local_heads = width // (2 * HD)
    positions = jnp.arange(stripe * shards, dtype=jnp.int32)
    owner_flat = owners[0].reshape(-1)
    length_flat = lengths[0].reshape(-1)
    source = (owner_flat[:, None] + positions[None, :] // stripe) % shards
    neighbour_index = jnp.arange(per_seq, dtype=jnp.int32)[:, None]
    flat_index = (source * per_seq + neighbour_index) * stripe + (positions % stripe)[None, :]
    key_value = arrived.reshape(-1, width)[flat_index]
    live = positions[None, :] < length_flat[:, None]
    spans = per_seq // KNN
    window = KNN * positions.shape[0]
    span_pairs = key_value.reshape(spans, window, width)
    span_live = live.reshape(spans, window)
    prior_pairs = jnp.concatenate(
        [jnp.zeros((1, window, width), jnp.bfloat16), span_pairs[:-1]], axis=0
    )
    prior_live = jnp.concatenate([jnp.zeros((1, window), bool), span_live[:-1]], axis=0)
    query_spans = queries.reshape(spans, SPAN, local_heads, HD)
    key_heads = prior_pairs[:, :, : local_heads * HD].reshape(spans, window, local_heads, HD)
    value_heads = prior_pairs[:, :, local_heads * HD :].reshape(spans, window, local_heads, HD)
    scores = jnp.einsum(
        "cqhd,ckhd->chqk", query_spans, key_heads, preferred_element_type=jnp.float32
    ) * HD ** (-0.5)
    masked = jnp.where(prior_live[:, None, None, :], scores, -jnp.inf)
    largest = jnp.max(masked, axis=-1, keepdims=True)
    largest = jnp.where(jnp.isfinite(largest), largest, 0.0)
    powers = jnp.exp(masked - largest)
    totals = jnp.sum(powers, axis=-1, keepdims=True)
    weights = (powers / jnp.where(totals > 0, totals, 1.0)).astype(jnp.bfloat16)
    attended = jnp.einsum(
        "chqk,ckhd->cqhd", weights, value_heads, preferred_element_type=jnp.float32
    )
    attended = attended.reshape(seq_len, local_heads * HD).astype(jnp.bfloat16)
    model_cols = output_part.shape[1]
    update = jnp.dot(
        lax.all_gather(attended, "seq", axis=1, tiled=True),
        output_part,
        preferred_element_type=jnp.float32,
    )
    residual = lax.dynamic_slice_in_dim(rows, seq_index * model_cols, model_cols, 1)
    result = (residual.astype(jnp.float32) + update).astype(jnp.bfloat16)
    return result[None]


MESH = pl.DeviceIdType.MESH
ZS, YS, XS = 4, 2, 2
PLANE = YS * XS
AHEAD = 2
LIMIT = 56 * 1024 * 1024


def remote(src, dst, send_sem, recv_sem, chip, core):
    return pltpu.make_async_remote_copy(
        src_ref=src,
        dst_ref=dst,
        send_sem=send_sem,
        recv_sem=recv_sem,
        device_id=(chip, core),
        device_id_type=MESH,
    )


def enter(chip, core, shards):
    barrier = pltpu.get_barrier_semaphore()
    for step in range(1, shards):
        pl.semaphore_signal(
            barrier, inc=1, device_id=(lax.rem(chip + step, shards), core), device_id_type=MESH
        )
    pl.semaphore_signal(barrier, inc=1, device_id=(chip, 1 - core), device_id_type=MESH)
    pl.semaphore_wait(barrier, shards)


def gather_kernel(
    ids, reader, database, encoder_w, pair_w, query_w, output_w,
    rows_out, arrived, encoder_all, pair_all, query_all, output_all,
    outgoing, z_send, z_recv, f_send, f_recv, s_send, s_recv,
    row_send, row_recv, pass_send, pass_recv, local_sem,
):
    shards = ZS * PLANE
    chip = lax.axis_index("db")
    core = lax.axis_index("seq")
    z, y, x = chip // PLANE, lax.rem(chip // XS, YS), lax.rem(chip, XS)

    def at(zz, yy, xx):
        return zz * PLANE + yy * XS + xx

    enter(chip, core, shards)

    shares = (encoder_w, pair_w, query_w, output_w)
    wholes = (encoder_all.at[core], pair_all, query_all, output_all)
    pieces = []
    for number, share in enumerate(shares):
        cut = share.shape[0] // 32 * 16
        pieces.append((number, 0, cut, True))
        pieces.append((number, cut, share.shape[0] - cut, False))

    def place(p, zz, yy, xx):
        number, low, count, _ = pieces[p]
        return wholes[number].at[zz, yy, xx, pl.ds(low, count)]

    def source(p):
        number, low, count, _ = pieces[p]
        return shares[number].at[pl.ds(low, count)]

    def line(p, yy, xx):
        number, low, count, _ = pieces[p]
        return wholes[number].at[:, yy, xx, pl.ds(low, count)]

    def peers(p):
        if pieces[p][3]:
            return (1 - y, x), (y, 1 - x)
        return (y, 1 - x), (1 - y, x)

    def along_z(p, step):
        return remote(
            source(p), place(p, z, y, x), z_send.at[p, step - 1], z_recv.at[p, step - 1],
            at(lax.rem(z + step, ZS), y, x), core,
        )

    def from_z(p, step):
        slot = place(p, lax.rem(z + ZS - step, ZS), y, x)
        return remote(slot, slot, z_send.at[p, step - 1], z_recv.at[p, step - 1], chip, 1 - core)

    def first(p, mine):
        here = (y, x) if mine else peers(p)[0]
        slots = line(p, *here)
        return remote(slots, slots, f_send.at[p], f_recv.at[p], at(z, *peers(p)[0]), core)

    def second(p, which, mine):
        toward = peers(p)[1]
        here = [(y, x), peers(p)[0]][which] if mine else [toward, (1 - y, 1 - x)][which]
        slots = line(p, *here)
        return remote(slots, slots, s_send.at[p, which], s_recv.at[p, which], at(z, *toward), core)

    own = []
    for number, share in enumerate(shares):
        copy = pltpu.make_async_copy(share, wholes[number].at[z, y, x], local_sem.at[number])
        copy.start()
        own.append(copy)
    kept = pltpu.make_async_copy(reader, rows_out.at[core], local_sem.at[4])
    kept.start()
    passed = remote(reader, rows_out.at[core], pass_send.at[0], pass_recv.at[0], chip, 1 - core)
    passed.start()

    for p in range(AHEAD):
        for step in range(1, ZS):
            along_z(p, step).start()
        if p == 0:
            per_row = ids.shape[0] // (2 * shards)
            for b in range(shards):
                base = (b * 2 + core) * per_row
                for m in range(per_row // KNN):
                    both = [database[ids[base + m * KNN + j]] for j in range(KNN)]
                    outgoing[b, m] = jnp.concatenate(both, axis=0)
            for step in range(1, shards):
                to = lax.rem(chip + step, shards)
                remote(
                    outgoing.at[to], arrived.at[:, chip], row_send.at[step - 1],
                    row_recv.at[step - 1], to, core,
                ).start()
            mine = pltpu.make_async_copy(outgoing.at[chip], arrived.at[:, chip], local_sem.at[5])
            mine.start()

    for copy in own:
        copy.wait()
    for p in range(len(pieces) + 1):
        if p < len(pieces):
            for step in range(1, ZS):
                from_z(p, step).wait_recv()
            first(p, True).start()
            second(p, 0, True).start()
            if p + AHEAD < len(pieces):
                for step in range(1, ZS):
                    along_z(p + AHEAD, step).start()
        if p > 0:
            first(p - 1, False).wait_recv()
            second(p - 1, 1, True).start()
    whole = encoder_all.at[core]
    for p in range(len(pieces)):
        for which in range(2):
            second(p, which, False).wait_recv()
        if p == 1:
            remote(whole, whole, pass_send.at[1], pass_recv.at[1], chip, 1 - core).start()

    for p in range(len(pieces)):
        for step in range(1, ZS):
            along_z(p, step).wait_send()
        first(p, True).wait_send()
        for which in range(2):
            second(p, which, True).wait_send()
    for step in range(1, shards):
        sender = lax.rem(chip + shards - step, shards)
        landed = remote(
            outgoing.at[sender], arrived.at[:, sender], row_send.at[step - 1],
            row_recv.at[step - 1], sender, core,
        )
        landed.wait_send()
        landed.wait_recv()
    mine.wait()
    kept.wait()
    other = rows_out.at[1 - core]
    taken = remote(other, other, pass_send.at[0], pass_recv.at[0], chip, 1 - core)
    taken.wait_send()
    taken.wait_recv()
    other = encoder_all.at[1 - core]
    taken = remote(other, other, pass_send.at[1], pass_recv.at[1], chip, 1 - core)
    taken.wait_send()
    taken.wait_recv()


def gather_all(ids, reader, database, encoder_w, pair_w, query_w, output_w):
    shards = ZS * PLANE
    bf16 = jnp.bfloat16
    features = database.shape[-1]
    per_row = ids.shape[0] // (2 * shards)
    spans = per_row // KNN
    stripes = KNN * database.shape[1]

    def whole(share):
        return jax.ShapeDtypeStruct((ZS, YS, XS) + share.shape, bf16)

    vmem, smem = pl.BlockSpec(memory_space=pltpu.VMEM), pl.BlockSpec(memory_space=pltpu.SMEM)
    hbm = pl.BlockSpec(memory_space=pl.ANY)
    dma = pltpu.SemaphoreType.DMA
    return pl.pallas_call(
        gather_kernel,
        out_shape=(
            jax.ShapeDtypeStruct((2,) + reader.shape, bf16),
            jax.ShapeDtypeStruct((spans, shards, stripes, features), bf16),
            jax.ShapeDtypeStruct((2, ZS, YS, XS) + encoder_w.shape, bf16),
            whole(pair_w),
            whole(query_w),
            whole(output_w),
        ),
        in_specs=[smem, hbm, vmem, hbm, hbm, hbm, hbm],
        out_specs=(hbm,) * 6,
        scratch_shapes=[
            pltpu.VMEM((shards, spans, stripes, features), bf16),
            dma((8, 3)), dma((8, 3)), dma((8,)), dma((8,)), dma((8, 2)), dma((8, 2)),
            dma((shards - 1,)), dma((shards - 1,)), dma((2,)), dma((2,)), dma((6,)),
        ],
        compiler_params=pltpu.CompilerParams(
            collective_id=0, has_side_effects=True, vmem_limit_bytes=LIMIT // 4
        ),
    )(ids, reader, database, encoder_w, pair_w, query_w, output_w)


def swap_kernel(mine, both, send_sem, recv_sem, local_sem):
    chip = lax.axis_index("db")
    core = lax.axis_index("seq")
    barrier = pltpu.get_barrier_semaphore()
    pl.semaphore_signal(barrier, inc=1, device_id=(chip, 1 - core), device_id_type=MESH)
    pl.semaphore_wait(barrier, 1)
    kept = pltpu.make_async_copy(mine, both.at[core], local_sem)
    kept.start()
    copy = remote(mine, both.at[core], send_sem, recv_sem, chip, 1 - core)
    copy.start()
    kept.wait()
    copy.wait()


def swap(mine, number):
    vmem = pl.BlockSpec(memory_space=pltpu.VMEM)
    return pl.pallas_call(
        swap_kernel,
        out_shape=jax.ShapeDtypeStruct((2,) + mine.shape, mine.dtype),
        in_specs=[vmem],
        out_specs=vmem,
        scratch_shapes=[pltpu.SemaphoreType.DMA] * 3,
        compiler_params=pltpu.CompilerParams(
            collective_id=number, has_side_effects=True, vmem_limit_bytes=LIMIT // 4
        ),
    )(mine)


def banded_body(
    reader,
    reader_gain,
    database,
    encoder_gain,
    w_expand,
    w_reduce,
    w_query,
    w_key,
    w_value,
    w_output,
    neighbour_ids,
    lengths,
    owners,
):
    f32, bf16 = jnp.float32, jnp.bfloat16
    shards = ZS * PLANE
    core = lax.axis_index("seq")
    stripe, features = database.shape[1:]
    head_cols, model_cols = w_query.shape[1], w_output.shape[1]
    band = w_expand.shape[0]
    encoder_w = jnp.concatenate([w_expand, w_reduce.T], axis=0)
    pair_w = jnp.concatenate([w_key, w_value], axis=0)
    rows, arrived, encoder_all, pair_all, query_all, output_all = gather_all(
        neighbour_ids.reshape(-1), reader[0], database, encoder_w, pair_w, w_query, w_output
    )
    rows = rows.reshape(-1, rows.shape[-1])
    encoder_all = encoder_all.reshape(2, shards, 2 * band, -1)
    stored = arrived.reshape(-1, features)
    normed_rows = rms_scale(stored, encoder_gain).astype(bf16)
    hidden_parts = []
    for part in range(2):
        expand = encoder_all[part, :, :band].reshape(shards * band, -1)
        product = jnp.dot(normed_rows, expand, preferred_element_type=f32)
        product = lax.optimization_barrier(product)
        hidden_parts.append(jax.nn.gelu(product, approximate=False).astype(bf16))
    hidden = lax.optimization_barrier(jnp.concatenate(hidden_parts, axis=1))
    reduce_t = jnp.concatenate(
        [encoder_all[part, :, band:].reshape(shards * band, -1) for part in range(2)], axis=1
    )
    total = lax.dot_general(hidden, reduce_t, (((1,), (1,)), ((), ())), preferred_element_type=f32)
    encoded = (stored.astype(f32) + total).astype(bf16)
    encoded = swap(encoded, 1).reshape(-1, features)

    spans = neighbour_ids.shape[1] * neighbour_ids.shape[2] // KNN
    window = encoded.shape[0] // spans
    encoded = encoded[: (spans - 1) * window]
    pair_all = pair_all.reshape(shards, 2 * band, -1)
    key_w = pair_all[:, :band].reshape(shards * band, -1)
    value_w = pair_all[:, band:].reshape(shards * band, -1)
    heads = head_cols // HD
    keys = jnp.dot(encoded, key_w, preferred_element_type=f32).astype(bf16)
    values = jnp.dot(encoded, value_w, preferred_element_type=f32).astype(bf16)
    normed_tokens = rms_scale(rows[SPAN:], reader_gain).astype(bf16)
    queries = jnp.dot(
        normed_tokens, query_all.reshape(-1, head_cols), preferred_element_type=f32
    ).astype(bf16)

    owner = owners[0].reshape(spans, 1, KNN, 1)
    length = lengths[0].reshape(spans, 1, KNN, 1)
    origin = jnp.arange(shards, dtype=jnp.int32)[None, :, None, None]
    offset = jnp.arange(stripe, dtype=jnp.int32)[None, None, None, :]
    position = lax.rem(origin - owner + shards, shards) * stripe + offset
    live = (position < length).reshape(spans, window)[: spans - 1]

    query_spans = queries.reshape(spans - 1, SPAN, heads, HD)
    key_heads = keys.reshape(spans - 1, window, heads, HD)
    value_heads = values.reshape(spans - 1, window, heads, HD)
    scores = jnp.einsum(
        "cqhd,ckhd->chqk", query_spans, key_heads, preferred_element_type=f32
    ) * HD ** (-0.5)
    masked = jnp.where(live[:, None, None, :], scores, -jnp.inf)
    largest = jnp.max(masked, axis=-1, keepdims=True)
    powers = jnp.exp(masked - largest)
    totals = jnp.sum(powers, axis=-1, keepdims=True)
    weights = (powers / totals).astype(bf16)
    attended = jnp.einsum("chqk,ckhd->cqhd", weights, value_heads, preferred_element_type=f32)
    attended = attended.reshape(-1, head_cols).astype(bf16)
    attended = swap(attended, 2)
    output_part = output_all.reshape(2, head_cols, model_cols)
    update = jnp.dot(attended[0], output_part[0], preferred_element_type=f32)
    update = update + jnp.dot(attended[1], output_part[1], preferred_element_type=f32)
    update = jnp.concatenate([jnp.zeros((SPAN, model_cols), f32), update], axis=0)
    residual = lax.dynamic_slice_in_dim(rows, core * model_cols, model_cols, 1)
    return (residual.astype(f32) + update).astype(bf16)[None]


def solution(mesh):
    in_specs = (
        P("db", "seq", None),
        P(),
        P("db", None, None),
        P(),
        P("db", "seq"),
        P("seq", "db"),
        P("db", "seq"),
        P("db", "seq"),
        P("db", "seq"),
        P("db", "seq"),
        P(),
        P("db", None, None),
        P("db", None, None),
    )
    out_specs = P("db", None, "seq")
    grid = (mesh.shape["db"], mesh.shape["seq"])
    body = banded_body if grid == (ZS * YS * XS, 2) else general_body
    return jax.shard_map(body, mesh=mesh, in_specs=in_specs, out_specs=out_specs, check_vma=False)
```
